512 devices in a mesh: width: 32 (over z, core), lat: 16 (over x, y).
Axes of the slice: x: 4, y: 4, z: 16, core: 2. Of those that a mesh axis runs over, the one named last changes fastest.
Arguments:
- residuals: bfloat16 [384, 16384], P(None, 'width'), may hold values from -6 to 6
- encoder: bfloat16 [16384, 16384], P('width', 'lat'), may hold values from -0.046875 to 0.046875
- enc_bias: float32 [16384], P('lat'), may hold values from -3 to 3
- decoder: bfloat16 [16384, 16384], P('lat', 'width'), may hold values from -0.046875 to 0.046875
- dec_bias: float32 [16384], P('width'), may hold values from -3 to 3
Outputs:
- enc_grad: bfloat16 [16384, 16384], P('width', 'lat')
- new_decoder: bfloat16 [16384, 16384], P('lat', 'width')
The draws below stay inside these ranges and needn't reach their ends.
All inputs are finite; a program needn't handle non-finite values.
Results may differ from the reference program's by a relative error of at most 0.011.
Values may be sent and summed in bfloat16 or wider, within the bound.
No kernel may reach another device: no remote copies, remote signals or barrier semaphores. Data moves between devices by JAX's collectives and lax.ppermute only.
A program may use at most 64 MiB of HBM per device.

```python
import jax
import jax.numpy as jnp
from jax import lax

D = 16384
TOK = 384
LATENTS = 16384
N_LAT = 16


def level_of(rng, shape, shards, least, top_value):
    loudness, own = 1.0, jax.random.fold_in(rng, 6)
    for position, blocks in shards:
        draws = jnp.exp(jax.random.uniform(jax.random.fold_in(own, position), (blocks,), jnp.float32, least / len(shards), top_value / len(shards)))
        loudness = loudness * jnp.repeat(draws, shape[position] // blocks).reshape([-1 if axis == position else 1 for axis in range(len(shape))])
    return loudness


def scatter_about(rng, dims, scale, most, cuts=(), held_as=jnp.bfloat16):
    result = jax.random.normal(rng, dims, jnp.float32) * scale
    if len(cuts) > 0:
        result = level_of(rng, dims, cuts, -0.22, 0.18) * result
    return jnp.clip(result, min=-most, max=most).astype(held_as)


def setup_inputs(seed: int = 0) -> dict:
    key_list = jax.random.split(jax.random.key(seed), 6)
    residuals = scatter_about(key_list[0], (TOK, D), 1.0, 6.0, ((1, 32),))
    encoder = scatter_about(key_list[1], (D, LATENTS), D ** -0.5, 0.046875, ((0, 32), (1, 16)))
    enc_bias = scatter_about(key_list[2], (LATENTS,), 0.5, 3.0, ((0, 16),), jnp.float32)
    decoder = scatter_about(key_list[3], (LATENTS, D), D ** -0.5, 0.046875, ((0, 16), (1, 32)))
    dec_bias = scatter_about(key_list[4], (D,), 0.5, 3.0, ((0, 32),), jnp.float32)
    return dict(residuals=residuals, encoder=encoder, enc_bias=enc_bias, decoder=decoder, dec_bias=dec_bias)


EPS = 1e-06
STEP = 0.0003
PENALTY = 0.5

def reference(residuals, encoder, enc_bias, decoder, dec_bias):
    pre = jnp.dot(residuals, encoder, preferred_element_type=jnp.float32) + enc_bias
    acts = jnp.maximum(pre, 0.0).astype(jnp.bfloat16)
    recon = jnp.dot(acts, decoder, preferred_element_type=jnp.float32)
    error = (recon + dec_bias - residuals.astype(jnp.float32)).astype(jnp.bfloat16)
    dacts = lax.dot_general(error, decoder, (((1,), (1,)), ((), ())), preferred_element_type=jnp.float32) + PENALTY
    dpre = jnp.where(pre > 0.0, dacts, 0.0).astype(jnp.bfloat16)
    enc_grad = lax.dot_general(residuals, dpre, (((0,), (0,)), ((), ())), preferred_element_type=jnp.float32).astype(jnp.bfloat16)
    blocks = N_LAT
    width = acts.shape[1] // blocks
    act_blocks = acts.reshape(acts.shape[0], blocks, width).transpose(1, 0, 2)
    dec_blocks = decoder.reshape(blocks, width, decoder.shape[1])

    def renorm(pair):
        act_blk, dec_blk = pair
        grad = lax.dot_general(act_blk, error, (((0,), (0,)), ((), ())), preferred_element_type=jnp.float32)
        weight = dec_blk.astype(jnp.float32)
        ww = lax.optimization_barrier(jnp.sum(weight * weight, axis=1, keepdims=True))
        gw = lax.optimization_barrier(jnp.sum(grad * weight, axis=1, keepdims=True))
        coef = gw / (ww + EPS)
        moved = weight - STEP * (grad - coef * weight)
        squared = lax.optimization_barrier(jnp.sum(moved * moved, axis=1, keepdims=True))
        return (moved / jnp.sqrt(squared + EPS)).astype(jnp.bfloat16)
    new_decoder = lax.map(renorm, (act_blocks, dec_blocks)).reshape(decoder.shape)
    return (enc_grad, new_decoder)
```

```python
import jax
import jax.numpy as jnp
from jax import lax
from jax.sharding import Mesh
from jax.sharding import PartitionSpec as P

WIDTH = ("zhi", "zlo", "core")
STAGES = ("core", "zlo", "zhi")
F32, BF16 = jnp.float32, jnp.bfloat16

EPS = 1e-06
STEP = 0.0003
PENALTY = 0.5


def dot(a, b, contract):
    return lax.dot_general(a, b, (contract, ((), ())), preferred_element_type=F32)


def exchange(tiles, axis):
    return lax.all_to_all(tiles, axis, split_axis=0, concat_axis=0, tiled=True)


def sum_at_owner(shard, axis, sent):
    count = lax.axis_size(axis)
    tiles = shard.astype(sent).reshape(count, shard.shape[0] // count, *shard.shape[1:])
    return exchange(tiles, axis).astype(F32).sum(axis=0)


def staged_sum(shard, sent):
    for axis in STAGES:
        shard = sum_at_owner(shard, axis, sent)
    return shard


def sent_to_all(shard, axis):
    count = lax.axis_size(axis)
    tiles = exchange(jnp.broadcast_to(shard[None], (count, *shard.shape)), axis)
    return tiles.reshape(-1, *shard.shape[1:])


def per_device(residuals, encoder, enc_bias, decoder, dec_bias):
    tokens = residuals.shape[0]
    latents = encoder.shape[1]
    lat_rows = tokens // lax.axis_size("lat")
    pre = staged_sum(dot(encoder, residuals, ((0,), (1,))), F32)
    own = pre.shape[0]
    place = (lax.axis_index("core") * 4 + lax.axis_index("zlo")) * 4 + lax.axis_index("zhi")
    pre = pre + lax.dynamic_slice_in_dim(enc_bias, place * own, own)[:, None]
    active = pre > 0.0
    act = jnp.maximum(pre, 0.0).astype(BF16)
    acts = lax.all_gather(act, STAGES, tiled=True)
    recon = sum_at_owner(dot(acts, decoder, ((0,), (0,))), "lat", BF16)
    first = lax.axis_index("lat") * lat_rows
    own_rows = lax.dynamic_slice_in_dim(residuals, first, lat_rows, 0)
    error_part = (recon + dec_bias - own_rows.astype(F32)).astype(BF16)
    error = sent_to_all(error_part, "lat")
    dacts = staged_sum(dot(decoder, error, ((1,), (1,))), BF16) + PENALTY
    dpre_part = jnp.where(active, dacts, 0.0).astype(BF16)
    grad = dot(acts, error, ((1,), (0,)))
    weight = decoder.astype(F32)
    stats = jnp.stack(
        (
            jnp.sum(weight * weight, axis=1),
            jnp.sum(grad * weight, axis=1),
            jnp.sum(grad * grad, axis=1),
        )
    ).reshape(-1, tokens)
    carried = lax.all_gather(jnp.concatenate((dpre_part, stats.astype(BF16))), STAGES)
    dpre = carried[:, :own].reshape(latents, tokens)
    ww, gw, gg = carried[:, own:].astype(F32).sum(axis=0).reshape(3, latents)
    enc_grad = dot(residuals, dpre, ((0,), (1,))).astype(BF16)
    coef_row = gw / (ww + EPS)
    coef = coef_row[:, None]
    moved = weight - STEP * (grad - coef * weight)
    squared = (
        ww
        - 2.0 * STEP * (gw - coef_row * ww)
        + STEP * STEP * (gg - 2.0 * coef_row * gw + coef_row * coef_row * ww)
    )
    new_decoder = (moved / jnp.sqrt(squared + EPS)[:, None]).astype(BF16)
    return (enc_grad, new_decoder)


def solution(mesh):
    finer = Mesh(
        mesh.devices.reshape(4, 4, 2, mesh.shape["lat"]), ("zhi", "zlo", "core", "lat")
    )
    placed = (P(None, WIDTH), P(WIDTH, "lat"), P("lat"), P("lat", WIDTH), P(WIDTH))
    return jax.shard_map(
        per_device,
        mesh=finer,
        in_specs=placed,
        out_specs=(P(WIDTH, "lat"), P("lat", WIDTH)),
        check_vma=False,
    )
```

```python
import jax
import jax.numpy as jnp
from jax import lax
from jax.sharding import Mesh
from jax.sharding import PartitionSpec as P

WIDTH = ("zhi", "zlo", "core")
STAGES = ("core", "zlo", "zhi")
F32, BF16 = jnp.float32, jnp.bfloat16

EPS = 1e-06
STEP = 0.0003
PENALTY = 0.5


def dot(a, b, contract):
    return lax.dot_general(a, b, (contract, ((), ())), preferred_element_type=F32)


def exchange(tiles, axis):
    return lax.all_to_all(tiles, axis, split_axis=0, concat_axis=0, tiled=True)


def sum_at_owner(shard, axis, sent):
    count = lax.axis_size(axis)
    tiles = shard.astype(sent).reshape(count, shard.shape[0] // count, *shard.shape[1:])
    return exchange(tiles, axis).astype(F32).sum(axis=0)


def staged_sum(shard, sent):
    sizes = [lax.axis_size(axis) for axis in WIDTH]
    tiles = shard.astype(sent).reshape(*sizes, -1, shard.shape[1])
    shard = tiles.transpose(2, 1, 0, 3, 4).reshape(shard.shape)
    for axis in STAGES:
        shard = sum_at_owner(shard, axis, sent)
    return shard


def sent_to_all(shard, axis):
    count = lax.axis_size(axis)
    tiles = exchange(jnp.broadcast_to(shard[None], (count, *shard.shape)), axis)
    return tiles.reshape(-1, *shard.shape[1:])


def per_device(residuals, encoder, enc_bias, decoder, dec_bias):
    tokens = residuals.shape[0]
    latents = encoder.shape[1]
    lat_rows = tokens // lax.axis_size("lat")
    pre = staged_sum(dot(encoder, residuals, ((0,), (1,))), F32)
    own = pre.shape[0]
    place = lax.axis_index(WIDTH)
    pre = pre + lax.dynamic_slice_in_dim(enc_bias, place * own, own)[:, None]
    active = pre > 0.0
    act = jnp.maximum(pre, 0.0).astype(BF16)
    acts = lax.all_gather(act, WIDTH, tiled=True)
    recon = sum_at_owner(dot(acts, decoder, ((0,), (0,))), "lat", BF16)
    first = lax.axis_index("lat") * lat_rows
    own_rows = lax.dynamic_slice_in_dim(residuals, first, lat_rows, 0)
    error_part = (recon + dec_bias - own_rows.astype(F32)).astype(BF16)
    error = sent_to_all(error_part, "lat")
    dacts = staged_sum(dot(decoder, error, ((1,), (1,))), BF16) + PENALTY
    dpre_part = jnp.where(active, dacts, 0.0).astype(BF16)
    grad = dot(acts, error, ((1,), (0,)))
    weight = decoder.astype(F32)
    stats = jnp.stack(
        (
            jnp.sum(weight * weight, axis=1),
            jnp.sum(grad * weight, axis=1),
            jnp.sum(grad * grad, axis=1),
        )
    ).reshape(-1, tokens)
    carried = lax.all_gather(jnp.concatenate((dpre_part, stats.astype(BF16))), WIDTH)
    dpre = carried[:, :own].reshape(latents, tokens)
    ww, gw, gg = carried[:, own:].astype(F32).sum(axis=0).reshape(3, latents)
    enc_grad = dot(residuals, dpre, ((0,), (1,))).astype(BF16)
    coef_row = gw / (ww + EPS)
    coef = coef_row[:, None]
    moved = weight - STEP * (grad - coef * weight)
    squared = (
        ww
        - 2.0 * STEP * (gw - coef_row * ww)
        + STEP * STEP * (gg - 2.0 * coef_row * gw + coef_row * coef_row * ww)
    )
    new_decoder = (moved / jnp.sqrt(squared + EPS)[:, None]).astype(BF16)
    return (enc_grad, new_decoder)


def solution(mesh):
    finer = Mesh(
        mesh.devices.reshape(4, 4, 2, mesh.shape["lat"]), ("zhi", "zlo", "core", "lat")
    )
    placed = (P(None, WIDTH), P(WIDTH, "lat"), P("lat"), P("lat", WIDTH), P(WIDTH))
    return jax.shard_map(
        per_device,
        mesh=finer,
        in_specs=placed,
        out_specs=(P(WIDTH, "lat"), P("lat", WIDTH)),
        check_vma=False,
    )
```

```python
import functools

import jax
import jax.numpy as jnp
from jax import lax
from jax.experimental import pallas as pl
from jax.experimental.pallas import tpu as pltpu
from jax.sharding import Mesh
from jax.sharding import PartitionSpec as P

WIDTH = ("zhi", "zlo", "core")
F32, BF16 = jnp.float32, jnp.bfloat16
LANES = 128

EPS = 1e-06
STEP = 0.0003
PENALTY = 0.5


def dot(a, b, contract):
    return lax.dot_general(a, b, (contract, ((), ())), preferred_element_type=F32)


def exchange(tiles, axis):
    return lax.all_to_all(tiles, axis, split_axis=0, concat_axis=0, tiled=True)


def sum_at_owner(shard, axis):
    count = lax.axis_size(axis)
    tiles = shard.reshape(count, shard.shape[0] // count, *shard.shape[1:])
    return exchange(tiles, axis).astype(F32).sum(axis=0)


def staged_sum(shard, stages, sent):
    for stage in stages:
        shard = sum_at_owner(shard.astype(sent), stage)
    return shard


def sent_to_all(shard, axis):
    count = lax.axis_size(axis)
    tiles = exchange(jnp.broadcast_to(shard[None], (count, *shard.shape)), axis)
    return tiles.reshape(-1, *shard.shape[1:])


def own_block(array, axis):
    rows = array.shape[0] // lax.axis_size(axis)
    return lax.dynamic_slice_in_dim(array, lax.axis_index(axis) * rows, rows, 0)


def whole_in_vmem(body, outs, operands, flops):
    size = sum(a.size * a.dtype.itemsize for a in (*operands, *outs))
    spec = pl.BlockSpec(memory_space=pltpu.VMEM)
    return pl.pallas_call(
        body,
        out_shape=outs,
        in_specs=[spec] * len(operands),
        out_specs=[spec] * len(outs),
        compiler_params=pltpu.CompilerParams(vmem_limit_bytes=16 * 2**20),
        cost_estimate=pl.CostEstimate(flops=flops, bytes_accessed=size, transcendentals=0),
    )(*operands)


def product_body(left, right, out):
    out[...] = dot(left[...], right[...], ((1,), (0,))).astype(out.dtype)


def dacts_body(decoder, error, out):
    cores, zs, own = out.shape[:3]
    step = 4
    for first in range(0, zs, step):
        rows = decoder[first * cores * own : (first + step) * cores * own, :]
        part = dot(rows, error[...], ((1,), (0,))).astype(BF16)
        for z in range(step):
            for core in range(cores):
                at = (z * cores + core) * own
                out[core, first + z] = part[at : at + own, :]


def grad_body(acts, error, decoder, grad, stats):
    for r in range(acts.shape[0] // LANES):
        rows = slice(r * LANES, (r + 1) * LANES)
        part = dot(acts[rows, :], error[...], ((1,), (1,)))
        grad[rows, :] = part
        weight = decoder[rows, :].astype(F32)
        for k, product in enumerate((weight * weight, part * weight, part * part)):
            folded = product[:, :LANES]
            for c in range(LANES, product.shape[1], LANES):
                folded = folded + product[:, c : c + LANES]
            line = jnp.sum(folded.T, axis=0, keepdims=True)
            stats[r : r + 1, k * LANES : (k + 1) * LANES] = line


def final_body(own, inputs, carried, stats, grad, decoder, enc_grad, new_decoder):
    count = carried.shape[0]
    step = 8
    for first in range(0, count, step):
        rows = carried[first : first + step, :own, :].reshape(step * own, carried.shape[2])
        columns = slice(first * own, (first + step) * own)
        enc_grad[:, columns] = dot(inputs[...], rows, ((1,), (1,))).astype(BF16)
    ww, gw, gg = (stats[:, k * LANES : (k + 1) * LANES] for k in range(3))
    coef = gw / (ww + EPS)
    squared = (
        ww
        - 2.0 * STEP * (gw - coef * ww)
        + STEP * STEP * (gg - 2.0 * coef * gw + coef * coef * ww)
    )
    scale = lax.rsqrt(squared + EPS)
    of_weight = scale * (1.0 + STEP * coef)
    of_grad = scale * STEP
    for r in range(stats.shape[0]):
        rows = slice(r * LANES, (r + 1) * LANES)
        a, b = (
            jnp.broadcast_to(t[r : r + 1, :], (LANES, LANES)).T for t in (of_weight, of_grad)
        )
        for c in range(0, grad.shape[1], LANES):
            at = (rows, slice(c, c + LANES))
            new_decoder[at] = (a * decoder[at].astype(F32) - b * grad[at]).astype(BF16)


def per_device(residuals, encoder, enc_bias, decoder, dec_bias):
    tokens, depth = residuals.shape
    latents = encoder.shape[1]
    sizes = [lax.axis_size(axis) for axis in WIDTH]
    own = latents // lax.axis_size(WIDTH)
    flops = 2 * tokens * depth * latents
    inputs, turned = lax.optimization_barrier((residuals.T, decoder.T))
    partial = dot(encoder, residuals, ((0,), (1,))).reshape(*sizes, own, tokens)
    partial = partial.transpose(2, 1, 0, 3, 4).reshape(latents, tokens)
    pre = staged_sum(partial, ("core", "zlo", "zhi"), F32)
    pre = pre + own_block(enc_bias, WIDTH)[:, None]
    active = pre > 0.0
    act = jnp.maximum(pre, 0.0).astype(BF16)
    acts = lax.all_gather(act, WIDTH, tiled=True)
    (recon,) = whole_in_vmem(
        product_body, [jax.ShapeDtypeStruct((depth, tokens), BF16)], (turned, acts), flops
    )
    recon = sum_at_owner(recon, "lat")
    target = own_block(inputs, "lat").astype(F32)
    error_part = (recon + own_block(dec_bias, "lat")[:, None] - target).astype(BF16)
    error = sent_to_all(error_part, "lat")
    zs = sizes[0] * sizes[1]
    (partial,) = whole_in_vmem(
        dacts_body,
        [jax.ShapeDtypeStruct((sizes[2], zs, own, tokens), BF16)],
        (decoder, error),
        flops,
    )
    dacts = staged_sum(partial.reshape(latents, tokens), ("core", ("zhi", "zlo")), BF16) + PENALTY
    dpre_part = jnp.where(active, dacts, 0.0).astype(BF16)
    groups = latents // LANES
    grad, stats = whole_in_vmem(
        grad_body,
        [
            jax.ShapeDtypeStruct((latents, depth), F32),
            jax.ShapeDtypeStruct((groups, 3 * LANES), F32),
        ],
        (acts, error, decoder),
        flops,
    )
    carried = lax.all_gather(jnp.concatenate((dpre_part, stats.astype(BF16))), WIDTH)
    stats = carried[:, own:].astype(F32).sum(axis=0)
    enc_grad, new_decoder = whole_in_vmem(
        functools.partial(final_body, own),
        [
            jax.ShapeDtypeStruct((depth, latents), BF16),
            jax.ShapeDtypeStruct((latents, depth), BF16),
        ],
        (inputs, carried, stats, grad, decoder),
        flops,
    )
    return (enc_grad, new_decoder)


def solution(mesh):
    finer = Mesh(
        mesh.devices.reshape(4, 4, 2, mesh.shape["lat"]), ("zhi", "zlo", "core", "lat")
    )
    placed = (P(None, WIDTH), P(WIDTH, "lat"), P("lat"), P("lat", WIDTH), P(WIDTH))
    return jax.shard_map(
        per_device,
        mesh=finer,
        in_specs=placed,
        out_specs=(P(WIDTH, "lat"), P("lat", WIDTH)),
        check_vma=False,
    )
```

```python
import functools

import jax
import jax.numpy as jnp
from jax import lax
from jax.experimental import pallas as pl
from jax.experimental.pallas import tpu as pltpu
from jax.sharding import Mesh
from jax.sharding import PartitionSpec as P

WIDTH = ("zhi", "zlo", "core")
NEAR = ("zlo", "core")
F32, BF16 = jnp.float32, jnp.bfloat16
LANES = 128

EPS = 1e-06
STEP = 0.0003
PENALTY = 0.5


def dot(a, b, contract):
    return lax.dot_general(a, b, (contract, ((), ())), preferred_element_type=F32)


def exchange(tiles, axis):
    return lax.all_to_all(tiles, axis, split_axis=0, concat_axis=0, tiled=True)


def total(tiles):
    result = tiles[0].astype(F32)
    for k in range(1, tiles.shape[0]):
        result = result + tiles[k].astype(F32)
    return result


def total_body(tiles, out):
    out[...] = total(tiles).astype(out.dtype)


def sum_of(tiles):
    out = jax.ShapeDtypeStruct(tiles.shape[1:], tiles.dtype)
    return whole_in_vmem(total_body, [out], [tiles], tiles.size)[0]


def split_exchange(shard, axis):
    count = lax.axis_size(axis)
    tiles = shard.reshape(count, shard.shape[0] // count, *shard.shape[1:])
    return exchange(tiles, axis)


def own_block(array, axis):
    rows = array.shape[0] // lax.axis_size(axis)
    return lax.dynamic_slice_in_dim(array, lax.axis_index(axis) * rows, rows, 0)


def whole_in_vmem(body, outs, operands, flops, scratch=()):
    size = sum(a.size * a.dtype.itemsize for a in (*operands, *outs))
    spec = pl.BlockSpec(memory_space=pltpu.VMEM)
    return pl.pallas_call(
        body,
        out_shape=outs,
        in_specs=[spec] * len(operands),
        out_specs=[spec] * len(outs),
        scratch_shapes=scratch,
        compiler_params=pltpu.CompilerParams(vmem_limit_bytes=16 * 2**20),
        cost_estimate=pl.CostEstimate(flops=flops, bytes_accessed=size, transcendentals=0),
    )(*operands)


def product_body(left, right, out):
    out[...] = dot(left[...], right[...], ((1,), (0,))).astype(out.dtype)


def act_body(tiles, bias, act, active):
    pre = total(tiles) + bias[...]
    act[...] = jnp.maximum(pre, 0.0).astype(BF16)
    active[...] = jnp.where(pre > 0.0, 1.0, 0.0)


def error_body(tiles, offset, out):
    error = (total(tiles) + offset[...]).astype(BF16)
    for k in range(out.shape[0]):
        out[k] = error


def dacts_body(decoder, error, out):
    cores, zs, own = out.shape[:3]
    for z in range(zs):
        rows = decoder[z * cores * own : (z + 1) * cores * own, :]
        part = dot(rows, error[...], ((1,), (0,))).astype(BF16)
        for core in range(cores):
            out[core, z] = part[core * own : (core + 1) * own, :]


def in_two(sums):
    high = sums.astype(BF16).astype(F32)
    return jnp.concatenate((high, sums - high)).astype(BF16)


def from_two(rows):
    half = rows.shape[0] // 2
    return rows[:half] + rows[half:]


def grad_body(acts, error, decoder, grad, stats, sums):
    for r in range(acts.shape[0] // LANES):
        rows = slice(r * LANES, (r + 1) * LANES)
        part = dot(acts[rows, :], error[...], ((1,), (1,)))
        grad[rows, :] = part
        weight = decoder[rows, :].astype(F32)
        for k, product in enumerate((weight * weight, part * weight, part * part)):
            folded = product[:, :LANES]
            for c in range(LANES, product.shape[1], LANES):
                folded = folded + product[:, c : c + LANES]
            line = jnp.sum(folded.T, axis=0, keepdims=True)
            sums[r : r + 1, k * LANES : (k + 1) * LANES] = line
    stats[...] = in_two(sums[...])


def joined_body(tiles, stats, out):
    own = tiles.shape[1]
    out[:own, :] = total(tiles).astype(BF16)
    out[own:, :] = stats[...]


def dpre_body(tiles, active, out):
    own = active.shape[0]
    sums = total(tiles)
    dacts = sums[:own] + PENALTY
    out[:own, :] = jnp.where(active[...] > 0.0, dacts, 0.0).astype(BF16)
    out[own:, :] = in_two(from_two(sums[own:]))


def final_body(own, inputs, carried, grad, decoder, enc_grad, new_decoder):
    count, _, tokens = carried.shape
    step = 2
    for first in range(0, count, step):
        rows = carried[first : first + step, :own, :].reshape(step * own, tokens)
        columns = slice(first * own, (first + step) * own)
        enc_grad[:, columns] = dot(inputs[...], rows, ((1,), (1,))).astype(BF16)
    stats = carried[0, own:, :].astype(F32)
    for k in range(1, count):
        stats = stats + carried[k, own:, :].astype(F32)
    stats = from_two(stats)
    ww, gw, gg = (stats[:, k * LANES : (k + 1) * LANES] for k in range(3))
    coef = gw / (ww + EPS)
    squared = (
        ww
        - 2.0 * STEP * (gw - coef * ww)
        + STEP * STEP * (gg - 2.0 * coef * gw + coef * coef * ww)
    )
    scale = lax.rsqrt(squared + EPS)
    of_weight = scale * (1.0 + STEP * coef)
    of_grad = scale * STEP
    for r in range(stats.shape[0]):
        rows = slice(r * LANES, (r + 1) * LANES)
        a, b = (
            jnp.broadcast_to(t[r : r + 1, :], (LANES, LANES)).T for t in (of_weight, of_grad)
        )
        for c in range(0, grad.shape[1], LANES):
            at = (rows, slice(c, c + LANES))
            new_decoder[at] = (a * decoder[at].astype(F32) - b * grad[at]).astype(BF16)


def per_device(residuals, encoder, enc_bias, decoder, dec_bias):
    tokens, depth = residuals.shape
    latents = encoder.shape[1]
    zs, cores = lax.axis_size("zlo"), lax.axis_size("core")
    own = latents // (zs * cores)
    flops = 2 * tokens * depth * latents
    shape = jax.ShapeDtypeStruct
    inputs, turned = lax.optimization_barrier((residuals.T, decoder.T))

    partial = dot(encoder, residuals, ((0,), (1,))).reshape(zs, cores, own, tokens)
    partial = partial.transpose(1, 0, 2, 3).reshape(latents, tokens)
    pre = sum_of(split_exchange(partial, "core"))
    pre = sum_of(split_exchange(pre, "zlo"))
    act, active = whole_in_vmem(
        act_body,
        [shape(pre.shape, BF16), shape(pre.shape, F32)],
        (lax.all_gather(pre, "zhi"), own_block(enc_bias, NEAR)[:, None]),
        pre.size,
    )
    acts = lax.all_gather(act, NEAR, tiled=True)

    (recon,) = whole_in_vmem(product_body, [shape((depth, tokens), BF16)], (turned, acts), flops)
    tiles = split_exchange(recon, "lat")
    offset = own_block(dec_bias, "lat")[:, None] - own_block(inputs, "lat").astype(F32)
    (copies,) = whole_in_vmem(
        error_body, [shape(tiles.shape, BF16)], (tiles, offset), tiles.size
    )
    error = exchange(copies, "lat").reshape(depth, tokens)

    (partial,) = whole_in_vmem(
        dacts_body, [shape((cores, zs, own, tokens), BF16)], (decoder, error), flops
    )
    grad, stats = whole_in_vmem(
        grad_body,
        [shape((latents, depth), F32), shape((2 * latents // LANES, 3 * LANES), BF16)],
        (acts, error, decoder),
        flops,
        [pltpu.VMEM((latents // LANES, 3 * LANES), F32)],
    )
    half = sum_of(exchange(partial.reshape(cores, zs * own, tokens), "core"))
    tiles = split_exchange(half, "zlo")
    both = shape((own + stats.shape[0], tokens), BF16)
    (joined,) = whole_in_vmem(joined_body, [both], (tiles, stats), tiles.size)
    (dpre,) = whole_in_vmem(
        dpre_body, [both], (lax.all_gather(joined, "zhi"), active), 4 * joined.size
    )
    carried = lax.all_gather(dpre, NEAR)
    enc_grad, new_decoder = whole_in_vmem(
        functools.partial(final_body, own),
        [shape((depth, latents), BF16), shape((latents, depth), BF16)],
        (inputs, carried, grad, decoder),
        flops,
    )
    return (enc_grad, new_decoder)


def solution(mesh):
    finer = Mesh(
        mesh.devices.reshape(4, 4, 2, mesh.shape["lat"]), ("zhi", "zlo", "core", "lat")
    )
    placed = (P(None, WIDTH), P(WIDTH, "lat"), P("lat"), P("lat", WIDTH), P(WIDTH))
    return jax.shard_map(
        per_device,
        mesh=finer,
        in_specs=placed,
        out_specs=(P(WIDTH, "lat"), P("lat", WIDTH)),
        check_vma=False,
    )
```

```python
import functools

import jax
import jax.numpy as jnp
from jax import lax
from jax.experimental import pallas as pl
from jax.experimental.pallas import tpu as pltpu
from jax.sharding import Mesh
from jax.sharding import PartitionSpec as P

WIDTH = ("zhi", "zlo", "core")
NEAR = ("zlo", "core")
F32, BF16 = jnp.float32, jnp.bfloat16
LANES = 128

EPS = 1e-06
STEP = 0.0003
PENALTY = 0.5


def dot(a, b, contract):
    return lax.dot_general(a, b, (contract, ((), ())), preferred_element_type=F32)


def exchange(tiles, axis):
    return lax.all_to_all(tiles, axis, split_axis=0, concat_axis=0, tiled=True)


def total(tiles):
    result = tiles[0].astype(F32)
    for k in range(1, tiles.shape[0]):
        result = result + tiles[k].astype(F32)
    return result


def total_body(tiles, out):
    out[...] = total(tiles).astype(out.dtype)


def sum_of(tiles, kept):
    out = jax.ShapeDtypeStruct(tiles.shape[1:], kept)
    return whole_in_vmem(total_body, [out], [tiles], tiles.size)[0]


def split_exchange(shard, axis):
    count = lax.axis_size(axis)
    tiles = shard.reshape(count, shard.shape[0] // count, *shard.shape[1:])
    return exchange(tiles, axis)


def own_block(array, axis):
    rows = array.shape[0] // lax.axis_size(axis)
    return lax.dynamic_slice_in_dim(array, lax.axis_index(axis) * rows, rows, 0)


def whole_in_vmem(body, outs, operands, flops, scratch=()):
    size = sum(a.size * a.dtype.itemsize for a in (*operands, *outs))
    spec = pl.BlockSpec(memory_space=pltpu.VMEM)
    return pl.pallas_call(
        body,
        out_shape=outs,
        in_specs=[spec] * len(operands),
        out_specs=[spec] * len(outs),
        scratch_shapes=scratch,
        compiler_params=pltpu.CompilerParams(vmem_limit_bytes=16 * 2**20),
        cost_estimate=pl.CostEstimate(flops=flops, bytes_accessed=size, transcendentals=0),
    )(*operands)


def product_body(left, right, out):
    out[...] = dot(left[...], right[...], ((1,), (0,))).astype(out.dtype)


def act_body(tiles, bias, act):
    act[...] = jnp.maximum(total(tiles) + bias[...], 0.0).astype(BF16)


def error_body(tiles, offset, out):
    error = (total(tiles) + offset[...]).astype(BF16)
    for k in range(out.shape[0]):
        out[k] = error


def dacts_body(kept, got, errors, out):
    core = lax.axis_index("core")
    part = dot(kept[...], errors[core], ((1,), (0,)))
    part = part + dot(got[...], errors[1 - core], ((1,), (0,)))
    out[...] = part.astype(BF16)


def in_two(sums):
    high = sums.astype(BF16).astype(F32)
    return jnp.concatenate((high, sums - high)).astype(BF16)


def from_two(rows):
    half = rows.shape[0] // 2
    return rows[:half] + rows[half:]


def grad_body(acts, error, decoder, grad, stats, sums):
    for r in range(acts.shape[0] // LANES):
        rows = slice(r * LANES, (r + 1) * LANES)
        part = dot(acts[rows, :], error[...], ((1,), (1,)))
        grad[rows, :] = part
        weight = decoder[rows, :].astype(F32)
        for k, product in enumerate((weight * weight, part * weight, part * part)):
            folded = product[:, :LANES]
            for c in range(LANES, product.shape[1], LANES):
                folded = folded + product[:, c : c + LANES]
            line = jnp.sum(folded.T, axis=0, keepdims=True)
            sums[r : r + 1, k * LANES : (k + 1) * LANES] = line
    stats[...] = in_two(sums[...])


def core_sum_body(tiles, exact, rounded):
    pre = total(tiles)
    rounded[...] = pre.astype(BF16)
    far, near, own = exact.shape[:3]
    for z in range(far):
        for k in range(near):
            at = (k * far + z) * own
            exact[z, k] = pre[at : at + own, :]


def joined_body(tiles, stats, pre, bias, out):
    own, extra = tiles.shape[1], stats.shape[0]
    out[:own, :] = total(tiles).astype(BF16)
    out[own : own + extra, :] = stats[...]
    out[own + extra :, :] = jnp.where(pre[...] + bias[...] > 0.0, 1.0, 0.0).astype(BF16)


def dpre_body(tiles, out):
    masked = tiles.shape[1] - out.shape[0]
    own = tiles.shape[0] * masked
    sums = total(tiles.at[:, : out.shape[0], :])
    for k in range(tiles.shape[0]):
        rows = slice(k * masked, (k + 1) * masked)
        active = tiles[k, out.shape[0] :, :].astype(F32) > 0.0
        out[rows, :] = jnp.where(active, sums[rows] + PENALTY, 0.0).astype(BF16)
    out[own:, :] = in_two(from_two(sums[own:]))


def final_body(own, inputs, carried, grad, decoder, enc_grad, new_decoder):
    count, _, tokens = carried.shape
    step = 2
    for first in range(0, count, step):
        rows = carried[first : first + step, :own, :].reshape(step * own, tokens)
        columns = slice(first * own, (first + step) * own)
        enc_grad[:, columns] = dot(inputs[...], rows, ((1,), (1,))).astype(BF16)
    stats = carried[0, own:, :].astype(F32)
    for k in range(1, count):
        stats = stats + carried[k, own:, :].astype(F32)
    stats = from_two(stats)
    ww, gw, gg = (stats[:, k * LANES : (k + 1) * LANES] for k in range(3))
    coef = gw / (ww + EPS)
    squared = (
        ww
        - 2.0 * STEP * (gw - coef * ww)
        + STEP * STEP * (gg - 2.0 * coef * gw + coef * coef * ww)
    )
    scale = lax.rsqrt(squared + EPS)
    of_weight = scale * (1.0 + STEP * coef)
    of_grad = scale * STEP
    for r in range(stats.shape[0]):
        rows = slice(r * LANES, (r + 1) * LANES)
        a, b = (
            jnp.broadcast_to(t[r : r + 1, :], (LANES, LANES)).T for t in (of_weight, of_grad)
        )
        for c in range(0, grad.shape[1], LANES):
            at = (rows, slice(c, c + LANES))
            new_decoder[at] = (a * decoder[at].astype(F32) - b * grad[at]).astype(BF16)


def per_device(residuals, encoder, enc_bias, decoder, dec_bias):
    tokens, depth = residuals.shape
    latents = encoder.shape[1]
    zs, cores = lax.axis_size("zlo"), lax.axis_size("core")
    own = latents // (zs * cores)
    flops = 2 * tokens * depth * latents
    shape = jax.ShapeDtypeStruct
    inputs, turned = lax.optimization_barrier((residuals.T, decoder.T))

    partial = dot(encoder, residuals, ((0,), (1,))).reshape(zs, cores, own, tokens)
    partial = partial.transpose(1, 0, 2, 3).reshape(latents, tokens)
    far = lax.axis_size("zhi")
    exact, rounded = whole_in_vmem(
        core_sum_body,
        [shape((far, zs, own // far, tokens), F32), shape((zs * own, tokens), BF16)],
        [split_exchange(partial, "core")],
        latents * tokens,
    )
    near_bias = own_block(enc_bias, NEAR)
    bias = near_bias[:, None]
    own_bias = own_block(near_bias, "zhi")[:, None]
    exact = lax.psum_scatter(
        exact.reshape(zs * own, tokens), ("zhi", "zlo"), scatter_dimension=0, tiled=True
    )
    grouped = decoder.reshape(zs, cores, own, depth)
    core = lax.axis_index("core")
    kept, sent = (
        lax.dynamic_index_in_dim(grouped, k, 1, False).reshape(zs * own, depth)
        for k in (core, cores - 1 - core)
    )
    got = lax.ppermute(sent, "core", [(k, cores - 1 - k) for k in range(cores)])
    offset = own_block(dec_bias, "lat")[:, None] - own_block(inputs, "lat").astype(F32)
    rounded = sum_of(split_exchange(rounded, "zlo"), BF16)
    rounded, offset, kept, got, bias, own_bias = lax.optimization_barrier(
        (rounded, offset, kept, got, bias, own_bias)
    )
    (act,) = whole_in_vmem(
        act_body,
        [shape(rounded.shape, BF16)],
        (lax.all_gather(rounded, "zhi"), bias),
        4 * rounded.size,
    )
    acts = lax.all_gather(act, NEAR, tiled=True)

    (recon,) = whole_in_vmem(product_body, [shape((depth, tokens), BF16)], (turned, acts), flops)
    tiles = split_exchange(recon, "lat")
    (copies,) = whole_in_vmem(
        error_body, [shape(tiles.shape, BF16)], (tiles, offset), tiles.size
    )
    error = exchange(copies, "lat").reshape(depth, tokens)

    error, exact = lax.optimization_barrier((error, exact))
    (half,) = whole_in_vmem(
        dacts_body,
        [shape((zs * own, tokens), BF16)],
        (kept, got, lax.all_gather(error, "core")),
        flops,
    )

    grad, stats = whole_in_vmem(
        grad_body,
        [shape((latents, depth), F32), shape((2 * latents // LANES, 3 * LANES), BF16)],
        (acts, error, decoder),
        flops,
        [pltpu.VMEM((latents // LANES, 3 * LANES), F32)],
    )
    tiles = split_exchange(half, "zlo")
    both = shape((own + stats.shape[0], tokens), BF16)
    everything = shape((both.shape[0] + own // far, tokens), BF16)
    (joined,) = whole_in_vmem(
        joined_body, [everything], (tiles, stats, exact, own_bias), tiles.size
    )
    (dpre,) = whole_in_vmem(
        dpre_body, [both], [lax.all_gather(joined, "zhi")], 4 * joined.size
    )
    carried = lax.all_gather(dpre, NEAR)
    enc_grad, new_decoder = whole_in_vmem(
        functools.partial(final_body, own),
        [shape((depth, latents), BF16), shape((latents, depth), BF16)],
        (inputs, carried, grad, decoder),
        flops,
    )
    return (enc_grad, new_decoder)


def solution(mesh):
    finer = Mesh(
        mesh.devices.reshape(4, 4, 2, mesh.shape["lat"]), ("zhi", "zlo", "core", "lat")
    )
    placed = (P(None, WIDTH), P(WIDTH, "lat"), P("lat"), P("lat", WIDTH), P(WIDTH))
    return jax.shard_map(
        per_device,
        mesh=finer,
        in_specs=placed,
        out_specs=(P(WIDTH, "lat"), P("lat", WIDTH)),
        check_vma=False,
    )
```

```python
import functools

import jax
import jax.numpy as jnp
from jax import lax
from jax.experimental import pallas as pl
from jax.experimental.pallas import tpu as pltpu
from jax.sharding import Mesh
from jax.sharding import PartitionSpec as P

WIDTH = ("zhi", "zlo", "core")
NEAR = ("zlo", "core")
F32, BF16 = jnp.float32, jnp.bfloat16
LANES = 128

EPS = 1e-06
STEP = 0.0003
PENALTY = 0.5


def dot(a, b, contract):
    return lax.dot_general(a, b, (contract, ((), ())), preferred_element_type=F32)


def exchange(tiles, axis):
    return lax.all_to_all(tiles, axis, split_axis=0, concat_axis=0, tiled=True)


def total(tiles):
    result = tiles[0].astype(F32)
    for k in range(1, tiles.shape[0]):
        result = result + tiles[k].astype(F32)
    return result


def total_body(tiles, out):
    out[...] = total(tiles).astype(out.dtype)


def sum_of(tiles, kept):
    out = jax.ShapeDtypeStruct(tiles.shape[1:], kept)
    return whole_in_vmem(total_body, [out], [tiles], tiles.size)[0]


def split_exchange(shard, axis):
    count = lax.axis_size(axis)
    tiles = shard.reshape(count, shard.shape[0] // count, *shard.shape[1:])
    return exchange(tiles, axis)


def own_block(array, axis):
    rows = array.shape[0] // lax.axis_size(axis)
    return lax.dynamic_slice_in_dim(array, lax.axis_index(axis) * rows, rows, 0)


def whole_in_vmem(body, outs, operands, flops, scratch=()):
    size = sum(a.size * a.dtype.itemsize for a in (*operands, *outs))
    spec = pl.BlockSpec(memory_space=pltpu.VMEM)
    return pl.pallas_call(
        body,
        out_shape=outs,
        in_specs=[spec] * len(operands),
        out_specs=[spec] * len(outs),
        scratch_shapes=scratch,
        compiler_params=pltpu.CompilerParams(vmem_limit_bytes=16 * 2**20),
        cost_estimate=pl.CostEstimate(flops=flops, bytes_accessed=size, transcendentals=0),
    )(*operands)


def product_body(left, right, out):
    out[...] = dot(left[...], right[...], ((1,), (0,))).astype(out.dtype)


def act_body(tiles, bias, act):
    act[...] = jnp.maximum(total(tiles) + bias[...], 0.0).astype(BF16)


def error_body(tiles, offset, out):
    error = (total(tiles) + offset[...]).astype(BF16)
    for k in range(out.shape[0]):
        out[k] = error


def dacts_body(kept, got, errors, out):
    core = lax.axis_index("core")
    part = dot(kept[...], errors[core], ((1,), (0,)))
    part = part + dot(got[...], errors[1 - core], ((1,), (0,)))
    out[...] = part.astype(BF16)


def in_two(sums):
    high = sums.astype(BF16).astype(F32)
    return jnp.concatenate((high, sums - high)).astype(BF16)


def from_two(rows):
    half = rows.shape[0] // 2
    return rows[:half] + rows[half:]


def grad_body(acts, error, decoder, grad, stats, sums):
    for r in range(acts.shape[0] // LANES):
        rows = slice(r * LANES, (r + 1) * LANES)
        part = dot(acts[rows, :], error[...], ((1,), (1,)))
        grad[rows, :] = part
        weight = decoder[rows, :].astype(F32)
        for k, product in enumerate((weight * weight, part * weight, part * part)):
            folded = product[:, :LANES]
            for c in range(LANES, product.shape[1], LANES):
                folded = folded + product[:, c : c + LANES]
            line = jnp.sum(folded.T, axis=0, keepdims=True)
            sums[r : r + 1, k * LANES : (k + 1) * LANES] = line
    stats[...] = in_two(sums[...])


def core_sum_body(tiles, exact, rounded):
    pre = total(tiles)
    rounded[...] = pre.astype(BF16)
    far, near, own = exact.shape[:3]
    for z in range(far):
        for k in range(near):
            at = (k * far + z) * own
            exact[z, k] = pre[at : at + own, :]


def joined_body(tiles, stats, pre, bias, out):
    own, extra = tiles.shape[1], stats.shape[0]
    out[:own, :] = total(tiles).astype(BF16)
    out[own : own + extra, :] = stats[...]
    out[own + extra :, :] = jnp.where(pre[...] + bias[...] > 0.0, 1.0, 0.0).astype(BF16)


def dpre_body(tiles, out):
    masked = tiles.shape[1] - out.shape[0]
    own = tiles.shape[0] * masked
    sums = total(tiles.at[:, : out.shape[0], :])
    for k in range(tiles.shape[0]):
        rows = slice(k * masked, (k + 1) * masked)
        active = tiles[k, out.shape[0] :, :].astype(F32) > 0.0
        out[rows, :] = jnp.where(active, sums[rows] + PENALTY, 0.0).astype(BF16)
    out[own:, :] = in_two(from_two(sums[own:]))


def final_body(own, inputs, carried, grad, decoder, enc_grad, new_decoder):
    count, _, tokens = carried.shape
    step = 2
    for first in range(0, count, step):
        rows = carried[first : first + step, :own, :].reshape(step * own, tokens)
        columns = slice(first * own, (first + step) * own)
        enc_grad[:, columns] = dot(inputs[...], rows, ((1,), (1,))).astype(BF16)
    stats = carried[0, own:, :].astype(F32)
    for k in range(1, count):
        stats = stats + carried[k, own:, :].astype(F32)
    stats = from_two(stats)
    ww, gw, gg = (stats[:, k * LANES : (k + 1) * LANES] for k in range(3))
    coef = gw / (ww + EPS)
    squared = (
        ww
        - 2.0 * STEP * (gw - coef * ww)
        + STEP * STEP * (gg - 2.0 * coef * gw + coef * coef * ww)
    )
    scale = lax.rsqrt(squared + EPS)
    of_weight = scale * (1.0 + STEP * coef)
    of_grad = scale * STEP
    for r in range(stats.shape[0]):
        rows = slice(r * LANES, (r + 1) * LANES)
        a, b = (
            jnp.broadcast_to(t[r : r + 1, :], (LANES, LANES)).T for t in (of_weight, of_grad)
        )
        for c in range(0, grad.shape[1], LANES):
            at = (rows, slice(c, c + LANES))
            new_decoder[at] = (a * decoder[at].astype(F32) - b * grad[at]).astype(BF16)


def per_device(residuals, encoder, enc_bias, decoder, dec_bias):
    tokens, depth = residuals.shape
    latents = encoder.shape[1]
    zs, cores = lax.axis_size("zlo"), lax.axis_size("core")
    own = latents // (zs * cores)
    flops = 2 * tokens * depth * latents
    shape = jax.ShapeDtypeStruct
    inputs, turned = lax.optimization_barrier((residuals.T, decoder.T))

    partial = dot(encoder, residuals, ((0,), (1,))).reshape(zs, cores, own, tokens)
    partial = partial.transpose(1, 0, 2, 3).reshape(latents, tokens)
    far = lax.axis_size("zhi")
    exact, rounded = whole_in_vmem(
        core_sum_body,
        [shape((far, zs, own // far, tokens), F32), shape((zs * own, tokens), BF16)],
        [split_exchange(partial, "core")],
        latents * tokens,
    )
    near_bias = own_block(enc_bias, NEAR)
    bias = near_bias[:, None]
    own_bias = own_block(near_bias, "zhi")[:, None]
    exact = lax.psum_scatter(
        exact.reshape(zs * own, tokens), ("zhi", "zlo"), scatter_dimension=0, tiled=True
    )
    grouped = decoder.reshape(zs, cores, own, depth)
    core = lax.axis_index("core")
    kept, sent = (
        lax.dynamic_index_in_dim(grouped, k, 1, False).reshape(zs * own, depth)
        for k in (core, cores - 1 - core)
    )
    got = lax.ppermute(sent, "core", [(k, cores - 1 - k) for k in range(cores)])
    offset = own_block(dec_bias, "lat")[:, None] - own_block(inputs, "lat").astype(F32)
    rounded = sum_of(split_exchange(rounded, "zlo"), BF16)
    rounded, offset, kept, got = lax.optimization_barrier((rounded, offset, kept, got))
    (act,) = whole_in_vmem(
        act_body,
        [shape(rounded.shape, BF16)],
        (lax.all_gather(rounded, "zhi"), bias),
        4 * rounded.size,
    )
    acts = lax.all_gather(act, NEAR, tiled=True)

    (recon,) = whole_in_vmem(product_body, [shape((depth, tokens), BF16)], (turned, acts), flops)
    tiles = split_exchange(recon, "lat")
    (copies,) = whole_in_vmem(
        error_body, [shape(tiles.shape, BF16)], (tiles, offset), tiles.size
    )
    error = exchange(copies, "lat").reshape(depth, tokens)

    (half,) = whole_in_vmem(
        dacts_body,
        [shape((zs * own, tokens), BF16)],
        (kept, got, lax.all_gather(error, "core")),
        flops,
    )

    grad, stats = whole_in_vmem(
        grad_body,
        [shape((latents, depth), F32), shape((2 * latents // LANES, 3 * LANES), BF16)],
        (acts, error, decoder),
        flops,
        [pltpu.VMEM((latents // LANES, 3 * LANES), F32)],
    )
    half, exact = lax.optimization_barrier((half, exact))
    tiles = split_exchange(half, "zlo")
    both = shape((own + stats.shape[0], tokens), BF16)
    everything = shape((both.shape[0] + own // far, tokens), BF16)
    (joined,) = whole_in_vmem(
        joined_body, [everything], (tiles, stats, exact, own_bias), tiles.size
    )
    (dpre,) = whole_in_vmem(
        dpre_body, [both], [lax.all_gather(joined, "zhi")], 4 * joined.size
    )
    carried = lax.all_gather(dpre, NEAR)
    enc_grad, new_decoder = whole_in_vmem(
        functools.partial(final_body, own),
        [shape((depth, latents), BF16), shape((latents, depth), BF16)],
        (inputs, carried, grad, decoder),
        flops,
    )
    return (enc_grad, new_decoder)


def solution(mesh):
    finer = Mesh(
        mesh.devices.reshape(4, 4, 2, mesh.shape["lat"]), ("zhi", "zlo", "core", "lat")
    )
    placed = (P(None, WIDTH), P(WIDTH, "lat"), P("lat"), P("lat", WIDTH), P(WIDTH))
    return jax.shard_map(
        per_device,
        mesh=finer,
        in_specs=placed,
        out_specs=(P(WIDTH, "lat"), P("lat", WIDTH)),
        check_vma=False,
    )
```

```python
import functools

import jax
import jax.numpy as jnp
from jax import lax
from jax.experimental import pallas as pl
from jax.experimental.pallas import tpu as pltpu
from jax.sharding import Mesh
from jax.sharding import PartitionSpec as P

WIDTH = ("zhi", "zlo", "core")
NEAR = ("zlo", "core")
F32, BF16 = jnp.float32, jnp.bfloat16
LANES = 128

EPS = 1e-06
STEP = 0.0003
PENALTY = 0.5


def dot(a, b, contract):
    return lax.dot_general(a, b, (contract, ((), ())), preferred_element_type=F32)


def exchange(tiles, axis):
    return lax.all_to_all(tiles, axis, split_axis=0, concat_axis=0, tiled=True)


def total(tiles):
    result = tiles[0].astype(F32)
    for k in range(1, tiles.shape[0]):
        result = result + tiles[k].astype(F32)
    return result


def total_body(tiles, out):
    out[...] = total(tiles).astype(out.dtype)


def sum_of(tiles, kept):
    out = jax.ShapeDtypeStruct(tiles.shape[1:], kept)
    return whole_in_vmem(total_body, [out], [tiles], tiles.size)[0]


def split_exchange(shard, axis):
    count = lax.axis_size(axis)
    tiles = shard.reshape(count, shard.shape[0] // count, *shard.shape[1:])
    return exchange(tiles, axis)


def own_block(array, axis):
    rows = array.shape[0] // lax.axis_size(axis)
    return lax.dynamic_slice_in_dim(array, lax.axis_index(axis) * rows, rows, 0)


def whole_in_vmem(body, outs, operands, flops, scratch=()):
    size = sum(a.size * a.dtype.itemsize for a in (*operands, *outs))
    spec = pl.BlockSpec(memory_space=pltpu.VMEM)
    return pl.pallas_call(
        body,
        out_shape=outs,
        in_specs=[spec] * len(operands),
        out_specs=[spec] * len(outs),
        scratch_shapes=scratch,
        compiler_params=pltpu.CompilerParams(vmem_limit_bytes=16 * 2**20),
        cost_estimate=pl.CostEstimate(flops=flops, bytes_accessed=size, transcendentals=0),
    )(*operands)


def pre_body(encoder, residuals, out, held, tokens, arrived, ready):
    cores, zs, own = out.shape[:3]
    wide = cores * own
    first = pltpu.make_async_copy(residuals, tokens, ready)
    first.start()
    copies = []
    for z in range(zs):
        at = (slice(None), pl.ds(z * wide, wide))
        copies.append(pltpu.make_async_copy(encoder.at[at], held.at[at], arrived.at[z]))
        copies[z].start()
    first.wait()
    for z in range(zs):
        copies[z].wait()
        columns = held[:, z * wide : (z + 1) * wide]
        part = dot(columns, tokens[...], ((0,), (1,)))
        for core in range(cores):
            out[core, z] = part[core * own : (core + 1) * own, :]


def product_body(left, right, out):
    out[...] = dot(left[...], right[...], ((1,), (0,))).astype(out.dtype)


def act_body(tiles, bias, act):
    act[...] = jnp.maximum(total(tiles) + bias[...], 0.0).astype(BF16)


def error_body(tiles, offset, out):
    error = (total(tiles) + offset[...]).astype(BF16)
    for k in range(out.shape[0]):
        out[k] = error


def dacts_body(kept, got, errors, out):
    core = lax.axis_index("core")
    part = dot(kept[...], errors[core], ((1,), (0,)))
    part = part + dot(got[...], errors[1 - core], ((1,), (0,)))
    out[...] = part.astype(BF16)


def in_two(sums):
    high = sums.astype(BF16).astype(F32)
    return jnp.concatenate((high, sums - high)).astype(BF16)


def from_two(rows):
    half = rows.shape[0] // 2
    return rows[:half] + rows[half:]


def grad_body(acts, error, decoder, grad, stats, sums):
    for r in range(acts.shape[0] // LANES):
        rows = slice(r * LANES, (r + 1) * LANES)
        part = dot(acts[rows, :], error[...], ((1,), (1,)))
        grad[rows, :] = part
        weight = decoder[rows, :].astype(F32)
        for k, product in enumerate((weight * weight, part * weight, part * part)):
            folded = product[:, :LANES]
            for c in range(LANES, product.shape[1], LANES):
                folded = folded + product[:, c : c + LANES]
            line = jnp.sum(folded.T, axis=0, keepdims=True)
            sums[r : r + 1, k * LANES : (k + 1) * LANES] = line
    stats[...] = in_two(sums[...])


def core_sum_body(tiles, exact, rounded):
    pre = total(tiles)
    rounded[...] = pre.astype(BF16)
    far, near, own = exact.shape[:3]
    for z in range(far):
        for k in range(near):
            at = (k * far + z) * own
            exact[z, k] = pre[at : at + own, :]


def joined_body(tiles, stats, pre, bias, out):
    own, extra = tiles.shape[1], stats.shape[0]
    out[:own, :] = total(tiles).astype(BF16)
    out[own : own + extra, :] = stats[...]
    out[own + extra :, :] = jnp.where(pre[...] + bias[...] > 0.0, 1.0, 0.0).astype(BF16)


def dpre_body(tiles, out):
    masked = tiles.shape[1] - out.shape[0]
    own = tiles.shape[0] * masked
    sums = total(tiles.at[:, : out.shape[0], :])
    for k in range(tiles.shape[0]):
        rows = slice(k * masked, (k + 1) * masked)
        active = tiles[k, out.shape[0] :, :].astype(F32) > 0.0
        out[rows, :] = jnp.where(active, sums[rows] + PENALTY, 0.0).astype(BF16)
    out[own:, :] = in_two(from_two(sums[own:]))


def final_body(own, inputs, carried, grad, decoder, enc_grad, new_decoder):
    count, _, tokens = carried.shape
    step = 2
    for first in range(0, count, step):
        rows = carried[first : first + step, :own, :].reshape(step * own, tokens)
        columns = slice(first * own, (first + step) * own)
        enc_grad[:, columns] = dot(inputs[...], rows, ((1,), (1,))).astype(BF16)
    stats = carried[0, own:, :].astype(F32)
    for k in range(1, count):
        stats = stats + carried[k, own:, :].astype(F32)
    stats = from_two(stats)
    ww, gw, gg = (stats[:, k * LANES : (k + 1) * LANES] for k in range(3))
    coef = gw / (ww + EPS)
    squared = (
        ww
        - 2.0 * STEP * (gw - coef * ww)
        + STEP * STEP * (gg - 2.0 * coef * gw + coef * coef * ww)
    )
    scale = lax.rsqrt(squared + EPS)
    of_weight = scale * (1.0 + STEP * coef)
    of_grad = scale * STEP
    for r in range(stats.shape[0]):
        rows = slice(r * LANES, (r + 1) * LANES)
        a, b = (
            jnp.broadcast_to(t[r : r + 1, :], (LANES, LANES)).T for t in (of_weight, of_grad)
        )
        for c in range(0, grad.shape[1], LANES):
            at = (rows, slice(c, c + LANES))
            new_decoder[at] = (a * decoder[at].astype(F32) - b * grad[at]).astype(BF16)


def per_device(residuals, encoder, enc_bias, decoder, dec_bias):
    tokens, depth = residuals.shape
    latents = encoder.shape[1]
    zs, cores = lax.axis_size("zlo"), lax.axis_size("core")
    own = latents // (zs * cores)
    flops = 2 * tokens * depth * latents
    shape = jax.ShapeDtypeStruct
    inputs, turned = lax.optimization_barrier((residuals.T, decoder.T))

    spec = pl.BlockSpec(memory_space=pltpu.HBM)
    partial = pl.pallas_call(
        pre_body,
        out_shape=shape((cores, zs, own, tokens), F32),
        in_specs=[spec, spec],
        out_specs=pl.BlockSpec(memory_space=pltpu.VMEM),
        scratch_shapes=[
            pltpu.VMEM(encoder.shape, BF16),
            pltpu.VMEM(residuals.shape, BF16),
            pltpu.SemaphoreType.DMA((zs,)),
            pltpu.SemaphoreType.DMA,
        ],
        compiler_params=pltpu.CompilerParams(vmem_limit_bytes=61 * 2**20),
        cost_estimate=pl.CostEstimate(
            flops=flops, bytes_accessed=2 * encoder.size, transcendentals=0
        ),
    )(encoder, residuals).reshape(latents, tokens)
    far = lax.axis_size("zhi")
    exact, rounded = whole_in_vmem(
        core_sum_body,
        [shape((far, zs, own // far, tokens), F32), shape((zs * own, tokens), BF16)],
        [split_exchange(partial, "core")],
        latents * tokens,
    )
    near_bias = own_block(enc_bias, NEAR)
    bias = near_bias[:, None]
    own_bias = own_block(near_bias, "zhi")[:, None]
    exact = lax.psum_scatter(
        exact.reshape(zs * own, tokens), ("zhi", "zlo"), scatter_dimension=0, tiled=True
    )
    grouped = decoder.reshape(zs, cores, own, depth)
    core = lax.axis_index("core")
    kept, sent = (
        lax.dynamic_index_in_dim(grouped, k, 1, False).reshape(zs * own, depth)
        for k in (core, cores - 1 - core)
    )
    got = lax.ppermute(sent, "core", [(k, cores - 1 - k) for k in range(cores)])
    offset = own_block(dec_bias, "lat")[:, None] - own_block(inputs, "lat").astype(F32)
    rounded = sum_of(split_exchange(rounded, "zlo"), BF16)
    rounded, offset, kept, got = lax.optimization_barrier((rounded, offset, kept, got))
    (act,) = whole_in_vmem(
        act_body,
        [shape(rounded.shape, BF16)],
        (lax.all_gather(rounded, "zhi"), bias),
        4 * rounded.size,
    )
    acts = lax.all_gather(act, NEAR, tiled=True)

    (recon,) = whole_in_vmem(product_body, [shape((depth, tokens), BF16)], (turned, acts), flops)
    tiles = split_exchange(recon, "lat")
    (copies,) = whole_in_vmem(
        error_body, [shape(tiles.shape, BF16)], (tiles, offset), tiles.size
    )
    error = exchange(copies, "lat").reshape(depth, tokens)

    (half,) = whole_in_vmem(
        dacts_body,
        [shape((zs * own, tokens), BF16)],
        (kept, got, lax.all_gather(error, "core")),
        flops,
    )

    grad, stats = whole_in_vmem(
        grad_body,
        [shape((latents, depth), F32), shape((2 * latents // LANES, 3 * LANES), BF16)],
        (acts, error, decoder),
        flops,
        [pltpu.VMEM((latents // LANES, 3 * LANES), F32)],
    )
    half, exact = lax.optimization_barrier((half, exact))
    tiles = split_exchange(half, "zlo")
    both = shape((own + stats.shape[0], tokens), BF16)
    everything = shape((both.shape[0] + own // far, tokens), BF16)
    (joined,) = whole_in_vmem(
        joined_body, [everything], (tiles, stats, exact, own_bias), tiles.size
    )
    (dpre,) = whole_in_vmem(
        dpre_body, [both], [lax.all_gather(joined, "zhi")], 4 * joined.size
    )
    carried = lax.all_gather(dpre, NEAR)
    enc_grad, new_decoder = whole_in_vmem(
        functools.partial(final_body, own),
        [shape((depth, latents), BF16), shape((latents, depth), BF16)],
        (inputs, carried, grad, decoder),
        flops,
    )
    return (enc_grad, new_decoder)


def solution(mesh):
    finer = Mesh(
        mesh.devices.reshape(4, 4, 2, mesh.shape["lat"]), ("zhi", "zlo", "core", "lat")
    )
    placed = (P(None, WIDTH), P(WIDTH, "lat"), P("lat"), P("lat", WIDTH), P(WIDTH))
    return jax.shard_map(
        per_device,
        mesh=finer,
        in_specs=placed,
        out_specs=(P(WIDTH, "lat"), P("lat", WIDTH)),
        check_vma=False,
    )
```
